256 devices in a mesh: src: 2 (over core), rows: 128 (over z, y, x).
Axes of the slice: x: 4, y: 4, z: 8, core: 2. Of those that a mesh axis runs over, the one named last changes fastest.
Arguments:
- slip_units: int32 [512, 2000], P(None, 'src'), may hold values from 0 to 15
- slip_scales: float32 [512, 16], P(None, 'src'), may hold values from 0.02 to 0.2
- green: bfloat16 [2000, 491520], P('src', 'rows'), may hold values from -0.08944272 to 0.08944272
- coast_gauges: int32 [16384, 8], replicated, may hold values from 0 to 2047
- coast_amps: float32 [16384, 8], replicated, may hold values from 0.05 to 0.3
- coast_counts: int32 [16384], replicated, may hold values from 1 to 8
Outputs:
- onshore: float32 [512, 16384], P('src', 'rows')
The draws below stay inside these ranges and needn't reach their ends.
Inputs may be any that keep to these rules, and one draw needn't show every extreme that they name: coast_gauges names gauges.
All inputs are finite; a program needn't handle non-finite values.
Results may differ from the reference program's by a relative error of at most 0.0039.
Values may be sent and summed in bfloat16 or wider, within the bound.
A program may use at most 64 MiB of HBM per device.

```python
import math
import jax
import jax.numpy as jnp
from jax import lax

U = 2000
NG = 2048
NT = 240
UBLK = 125
K = 8
S = 512
NBLK = 16
TILES = 16384
N_SRC = 2
N_ROWS = 128


def draw_green(key, part):
    base_key = jax.random.fold_in(jax.random.fold_in(key, 7), 0)
    limit = 4.0 / math.sqrt(U)
    values = jax.random.normal(base_key, (U, NG * NT), jnp.float32) * (1.0 / math.sqrt(U))
    values = jnp.clip(values, -limit, limit)
    return values.astype(jnp.bfloat16)


def with_ends(result, stream_key, least, top_value):
    index_at = [jax.random.randint(jax.random.fold_in(stream_key, axis), (), 0, length) for axis, length in enumerate(result.shape)]
    main_axis = result.shape.index(max(result.shape))
    beside = index_at[:main_axis] + [(index_at[main_axis] + 1) % result.shape[main_axis]] + index_at[main_axis + 1:]
    return result.at[tuple(index_at)].set(least).at[tuple(beside)].set(top_value)


def steps_of(stream_key, extent, pieces, least, high):
    def one(dim, shards_of):
        heights = jax.random.uniform(jax.random.fold_in(jax.random.fold_in(stream_key, 6), dim), (shards_of,), jnp.float32, least / len(pieces), high / len(pieces))
        return jnp.repeat(jnp.exp(heights), extent[dim] // shards_of).reshape((-1,) + (1,) * (len(extent) - dim - 1))

    level = one(*pieces[0])
    for cut in pieces[1:]:
        level = level * one(*cut)
    return level


def setup_inputs(seed: int = 0) -> dict:
    seeds = jax.random.split(jax.random.key(seed), 7)
    slip_units = with_ends(jax.random.randint(seeds[0], (S, U), 0, 16), jax.random.fold_in(seeds[0], 1), 0, 15).astype(jnp.int32)
    slip_scales = jnp.clip(jnp.exp(math.log(0.2) - 2.3025851 * jax.random.uniform(seeds[1], (S, NBLK), jnp.float32) ** steps_of(seeds[1], (S, NBLK), ((1, 2),), -0.2, 0.2)), 0.02, 0.2)
    green = draw_green(jax.random.fold_in(seeds[6], 71), 0)
    coast_gauges = with_ends(jax.random.randint(seeds[3], (TILES, K), 0, NG), jax.random.fold_in(seeds[3], 1), 0, NG - 1).astype(jnp.int32)
    coast_amps = jnp.clip(jax.random.uniform(seeds[4], (TILES, K), jnp.float32, 0.05, 0.3), 0.05, 0.3)
    coast_counts = with_ends(jax.random.randint(seeds[5], (TILES,), 1, K + 1), jax.random.fold_in(seeds[5], 1), 1, K).astype(jnp.int32)
    return {"slip_units": slip_units, "slip_scales": slip_scales, "green": green, "coast_gauges": coast_gauges, "coast_amps": coast_amps, "coast_counts": coast_counts}


def reference(slip_units, slip_scales, green, coast_gauges, coast_amps, coast_counts):
    slip_weights = (slip_units.astype(jnp.float32).reshape(S, NBLK, UBLK) * slip_scales[:, :, None]).reshape(S, U).astype(jnp.bfloat16)
    group_size = U // N_SRC
    gauge_share = NG // N_ROWS
    column_share = gauge_share * NT

    def gauge_block(slab_index):
        column_block = lax.dynamic_slice_in_dim(green, slab_index * column_share, column_share, 1)
        summed = jnp.zeros((S, column_share), jnp.float32)
        for group in range(N_SRC):
            partial_value = jnp.dot(slip_weights[:, group * group_size:(group + 1) * group_size], column_block[group * group_size:(group + 1) * group_size], preferred_element_type=jnp.float32)
            rounded = lax.optimization_barrier(partial_value.astype(jnp.bfloat16))
            summed = summed + rounded.astype(jnp.float32)
        return jnp.max(jnp.abs(summed.reshape(S, gauge_share, NT)), axis=2)

    blocks = lax.map(gauge_block, jnp.arange(N_ROWS, dtype=jnp.int32))
    peak_values = jnp.transpose(blocks, (1, 0, 2)).reshape(S, NG)
    active_slot = jnp.arange(K, dtype=jnp.int32)[None, :] < coast_counts[:, None]
    weights = jnp.where(active_slot, coast_amps, jnp.zeros_like(coast_amps))
    picked = peak_values[:, coast_gauges]
    return jnp.sum(picked * weights[None, :, :], axis=2)
```

```python
import functools

import jax
import jax.numpy as jnp
from jax import lax
from jax.experimental import pallas as pl
from jax.experimental.pallas import tpu as pltpu
from jax.sharding import PartitionSpec as P

NT = 240
UBLK = 125
NX, NY, NZ = 4, 4, 8
CHUNKS = 5
BF16 = jnp.bfloat16
F32 = jnp.float32
MESH = pl.DeviceIdType.MESH


def gauge_peaks(tiles, first, gauges, lane):
    peaks = []
    for g in range(first, first + gauges):
        start, end = g * NT, (g + 1) * NT
        best = None
        for tile in range(start // 128, (end + 127) // 128):
            value = tiles(tile)
            lo, hi = start - tile * 128, end - tile * 128
            if lo > 0:
                value = jnp.where(lane >= lo, value, jnp.zeros_like(value))
            if hi < 128:
                value = jnp.where(lane < hi, value, jnp.zeros_like(value))
            best = value if best is None else jnp.maximum(best, value)
        peaks.append(best)
    return peaks


def kernel(
    units_hbm, scales_ref, green_hbm, gauges_hbm, amps_hbm, counts_ref,
    out_ref,
    units, green, slip, own, outgoing, incoming, gathered, table,
    gauges, amps,
    load_sem, pair_send, pair_recv, z_send, z_recv, a_send, a_recv, b_send, b_recv,
):
    core = lax.axis_index("src")
    rank = lax.axis_index("rows")
    sources, columns = green.shape
    half = slip.shape[0] // 2
    width = columns // CHUNKS
    here = columns // NT
    tiles_here = out_ref.shape[1]
    total = gathered.shape[0]
    x, y, z = rank % NX, (rank // NX) % NY, rank // (NX * NY)
    a = jnp.where(core == 0, x, y)
    b = jnp.where(core == 0, y, x)

    def at(a_index, b_index, z_index):
        x_index = jnp.where(core == 0, a_index, b_index)
        y_index = jnp.where(core == 0, b_index, a_index)
        return (core, (z_index * NY + y_index) * NX + x_index)

    barrier = pltpu.get_barrier_semaphore()
    partners = [(1 - core, rank)]
    partners += [at(a, b, (z + d) % NZ) for d in range(1, NZ)]
    partners += [at((a + d) % NX, b, z) for d in range(1, NX)]
    partners += [at(a, (b + d) % NY, z) for d in range(1, NY)]
    for partner in partners:
        pl.semaphore_signal(barrier, inc=1, device_id=partner, device_id_type=MESH)

    loads = []
    load_units = pltpu.make_async_copy(units_hbm, units, load_sem.at[0])
    load_units.start()
    for n in range(CHUNKS):
        cols = pl.ds(n * width, width)
        copy = pltpu.make_async_copy(green_hbm.at[:, cols], green.at[:, cols], load_sem.at[1 + n])
        copy.start()
        loads.append(copy)
    tile_cols = pl.ds(pl.multiple_of(rank * tiles_here, 128), tiles_here)
    load_gauges = pltpu.make_async_copy(gauges_hbm.at[:, tile_cols], gauges, load_sem.at[1 + CHUNKS])
    load_amps = pltpu.make_async_copy(amps_hbm.at[:, tile_cols], amps, load_sem.at[2 + CHUNKS])
    load_gauges.start()
    load_amps.start()

    load_units.wait()
    blocks = scales_ref.shape[0]
    for i in range(blocks):
        low, high = i * 128, min(i * 128 + 128, sources)
        scale = scales_ref[i : i + 1, :]
        if i + 1 < blocks:
            row = lax.broadcasted_iota(jnp.int32, (high - low, 1), 0) + low
            scale = jnp.where(row < UBLK * (i + 1), scale, scales_ref[i + 1 : i + 2, :])
        piece = units[low:high, :].astype(F32) * scale
        slip[:, low:high] = piece.astype(BF16).T

    pair = []
    mine = pl.ds(pl.multiple_of(core * half, half), half)
    other = pl.ds(pl.multiple_of((1 - core) * half, half), half)
    for n in range(CHUNKS):
        cols = pl.ds(n * width, width)
        loads[n].wait()
        outgoing[:, cols] = jnp.dot(
            slip[other, :], green[:, cols], preferred_element_type=F32
        ).astype(BF16)
        if n == 0:
            pl.semaphore_wait(barrier, len(partners))
        copy = pltpu.make_async_remote_copy(
            src_ref=outgoing.at[:, cols],
            dst_ref=incoming.at[:, cols],
            send_sem=pair_send.at[n],
            recv_sem=pair_recv.at[n],
            device_id=(1 - core, rank),
            device_id_type=MESH,
        )
        copy.start()
        pair.append(copy)
        own[:, cols] = jnp.dot(
            slip[mine, :], green[:, cols], preferred_element_type=F32
        ).astype(BF16)

    load_gauges.wait()
    load_amps.wait()
    slots = gauges.shape[0]
    listed = gauges[...]
    owner = listed >> 4
    gauge_z = owner >> 4
    gauge_y = (owner >> 2) & 3
    gauge_x = owner & 3
    gauge_a = jnp.where(core == 0, gauge_x, gauge_y)
    gauge_b = jnp.where(core == 0, gauge_y, gauge_x)
    place = (((gauge_b * 4 + gauge_a) * 8 + gauge_z) * 16 + (listed & 15)).T
    slot = lax.broadcasted_iota(jnp.int32, (slots, 1), 0)
    count = counts_ref[pl.ds(rank, 1), :]
    weight = jnp.where(slot < count, amps[...], 0.0).T
    step = 256

    def fill(i, carry):
        first = pl.multiple_of(i * step, step)
        position = lax.broadcasted_iota(jnp.int32, (tiles_here, step), 1) + first
        value = jnp.zeros((tiles_here, step), F32)
        for k in range(slots):
            value += jnp.where(place[:, k : k + 1] == position, weight[:, k : k + 1], 0.0)
        high = value.astype(BF16)
        table[0:tiles_here, pl.ds(first, step)] = high
        table[tiles_here : 2 * tiles_here, pl.ds(first, step)] = (value - high.astype(F32)).astype(BF16)
        return carry

    lax.fori_loop(0, total // step, fill, 0)

    for copy in pair:
        copy.wait_recv()
    lane = lax.broadcasted_iota(jnp.int32, (half, 128), 1)

    def tiles(i):
        cols = pl.ds(i * 128, 128)
        return jnp.abs(own[:, cols].astype(F32) + incoming[:, cols].astype(F32))

    rows = []
    for best in gauge_peaks(tiles, 0, here, lane):
        rows.append(jnp.max(best.T, axis=0, keepdims=True))
    first = ((b * NX + a) * NZ + z) * here
    block = pl.ds(pl.multiple_of(first, here), here)
    gathered[block, :] = jnp.concatenate(rows, axis=0).astype(BF16)

    sent = []

    def spread(size, count, start_of, partner_of, send_sem, recv_sem):
        source = gathered.at[pl.ds(pl.multiple_of(start_of(0), size), size), :]
        copies = []
        for d in range(1, count):
            copy = pltpu.make_async_remote_copy(
                src_ref=source,
                dst_ref=source,
                send_sem=send_sem.at[d - 1],
                recv_sem=recv_sem.at[d - 1],
                device_id=partner_of(d),
                device_id_type=MESH,
            )
            copy.start()
            sent.append(copy)
        for d in range(1, count):
            landed = gathered.at[pl.ds(pl.multiple_of(start_of(-d), size), size), :]
            copies.append(
                pltpu.make_async_remote_copy(
                    src_ref=landed,
                    dst_ref=landed,
                    send_sem=send_sem.at[d - 1],
                    recv_sem=recv_sem.at[d - 1],
                    device_id=partner_of(d),
                    device_id_type=MESH,
                )
            )
        return copies

    arrivals = spread(
        here, NZ, lambda d: ((b * NX + a) * NZ + (z + d + NZ) % NZ) * here,
        lambda d: at(a, b, (z + d) % NZ), z_send, z_recv,
    )
    for copy in arrivals:
        copy.wait_recv()
    size = here * NZ
    arrivals = spread(
        size, NX, lambda d: (b * NX + (a + d + NX) % NX) * size,
        lambda d: at((a + d) % NX, b, z), a_send, a_recv,
    )
    for copy in arrivals:
        copy.wait_recv()
    size = size * NX
    arrivals = spread(
        size, NY, lambda d: ((b + d + NY) % NY) * size,
        lambda d: at(a, (b + d) % NY, z), b_send, b_recv,
    )
    for copy in arrivals:
        copy.wait_recv()

    both = jnp.dot(table[...], gathered[...], preferred_element_type=F32)
    out_ref[...] = (both[:tiles_here] + both[tiles_here:]).T
    for copy in pair + sent:
        copy.wait_send()


def body(slip_units, slip_scales, green, coast_gauges, coast_amps, coast_counts):
    scenarios, sources = slip_units.shape
    columns = green.shape[1]
    tile_total, slots = coast_gauges.shape
    owners = lax.axis_size("rows")
    tiles_here = tile_total // owners
    half = scenarios // lax.axis_size("src")
    total = columns // NT * owners
    hbm = pl.BlockSpec(memory_space=pl.ANY)
    vmem = pl.BlockSpec(memory_space=pltpu.VMEM)
    dma = pltpu.SemaphoreType.DMA
    return pl.pallas_call(
        kernel,
        out_shape=jax.ShapeDtypeStruct((half, tiles_here), F32),
        in_specs=[hbm, vmem, hbm, hbm, hbm, vmem],
        out_specs=vmem,
        scratch_shapes=[
            pltpu.VMEM((sources, scenarios), jnp.int32),
            pltpu.VMEM((sources, columns), BF16),
            pltpu.VMEM((scenarios, sources), BF16),
            pltpu.VMEM((half, columns), BF16),
            pltpu.VMEM((half, columns), BF16),
            pltpu.VMEM((half, columns), BF16),
            pltpu.VMEM((total, half), BF16),
            pltpu.VMEM((2 * tiles_here, total), BF16),
            pltpu.VMEM((slots, tiles_here), jnp.int32),
            pltpu.VMEM((slots, tiles_here), F32),
            dma((3 + CHUNKS,)),
            dma((CHUNKS,)),
            dma((CHUNKS,)),
            dma((NZ - 1,)),
            dma((NZ - 1,)),
            dma((NX - 1,)),
            dma((NX - 1,)),
            dma((NY - 1,)),
            dma((NY - 1,)),
        ],
        compiler_params=pltpu.CompilerParams(
            collective_id=0, has_side_effects=True, vmem_limit_bytes=56 * 1024 * 1024
        ),
    )(
        slip_units.T,
        slip_scales.T,
        green,
        coast_gauges.T,
        coast_amps.T,
        coast_counts.reshape(owners, tiles_here),
    )


def solution(mesh):
    in_specs = (P(None, "src"), P(None, "src"), P("src", "rows"), P(), P(), P())
    out_specs = P("src", "rows")
    return jax.shard_map(body, mesh=mesh, in_specs=in_specs, out_specs=out_specs, check_vma=False)
```

```python
import functools

import jax
import jax.numpy as jnp
from jax import lax
from jax.experimental import pallas as pl
from jax.experimental.pallas import tpu as pltpu
from jax.sharding import PartitionSpec as P

NT = 240
UBLK = 125
NX, NY, NZ = 4, 4, 8
NS_AXIS, NT_AXIS = 4, 4
DZ_ORDER = (4, 3, 5, 2, 6, 1, 7, 0)
CHUNKS = 5
HELD = 3
BF16 = jnp.bfloat16
F32 = jnp.float32
MESH = pl.DeviceIdType.MESH


def gauge_peaks(tiles, first, gauges, lane):
    peaks = []
    for g in range(first, first + gauges):
        start, end = g * NT, (g + 1) * NT
        best = None
        for tile in range(start // 128, (end + 127) // 128):
            value = tiles(tile)
            lo, hi = start - tile * 128, end - tile * 128
            if lo > 0:
                value = jnp.where(lane >= lo, value, jnp.zeros_like(value))
            if hi < 128:
                value = jnp.where(lane < hi, value, jnp.zeros_like(value))
            best = value if best is None else jnp.maximum(best, value)
        peaks.append(best)
    return peaks


def kernel(
    units_hbm, scales_ref, green_hbm, gauges_hbm, amps_hbm, counts_ref,
    out_ref,
    units, green, slip, own, outgoing, incoming, peaks, gathered, table,
    gauges, amps,
    load_sem, pair_send, pair_recv, plane_send, plane_recv, line_send, line_recv,
):
    core = lax.axis_index("src")
    rank = lax.axis_index("rows")
    sources, columns = green.shape
    half = slip.shape[0] // 2
    width = columns // CHUNKS
    here = columns // NT
    tiles_here = out_ref.shape[1]
    total = gathered.shape[0]
    x, y, z = rank % NX, (rank // NX) % NY, rank // (NX * NY)
    s = jnp.where(core == 0, x, y)
    t = jnp.where(core == 0, y, x)

    def at(s_index, t_index, z_index):
        x_index = jnp.where(core == 0, s_index, t_index)
        y_index = jnp.where(core == 0, t_index, s_index)
        return (core, (z_index * NY + y_index) * NX + x_index)

    load_units = pltpu.make_async_copy(units_hbm, units, load_sem.at[0])
    load_units.start()
    loads = []
    for n in range(CHUNKS):
        cols = pl.ds(n * width, width)
        copy = pltpu.make_async_copy(green_hbm.at[:, cols], green.at[:, cols], load_sem.at[1 + n])
        copy.start()
        loads.append(copy)
    tile_cols = pl.ds(pl.multiple_of(rank * tiles_here, 128), tiles_here)
    load_gauges = pltpu.make_async_copy(gauges_hbm.at[:, tile_cols], gauges, load_sem.at[1 + CHUNKS])
    load_amps = pltpu.make_async_copy(amps_hbm.at[:, tile_cols], amps, load_sem.at[2 + CHUNKS])
    load_gauges.start()
    load_amps.start()

    barrier = pltpu.get_barrier_semaphore()
    sibling = (1 - core, rank)
    plane = [
        at(s, (t + dt) % NT_AXIS, (z + dz) % NZ)
        for dz in DZ_ORDER for dt in range(NT_AXIS) if dz or dt
    ]
    line = [at((s + d) % NS_AXIS, t, z) for d in range(1, NS_AXIS)]
    partners = [sibling] + plane + line
    for partner in partners:
        pl.semaphore_signal(barrier, inc=1, device_id=partner, device_id_type=MESH)

    load_units.wait()
    blocks = scales_ref.shape[0]
    for i in range(blocks):
        low, high = i * 128, min(i * 128 + 128, sources)
        scale = scales_ref[i : i + 1, :]
        if i + 1 < blocks:
            row = lax.broadcasted_iota(jnp.int32, (high - low, 1), 0) + low
            scale = jnp.where(row < UBLK * (i + 1), scale, scales_ref[i + 1 : i + 2, :])
        piece = units[low:high, :].astype(F32) * scale
        slip[:, low:high] = piece.astype(BF16).T

    mine = pl.ds(pl.multiple_of(core * half, half), half)
    other = pl.ds(pl.multiple_of((1 - core) * half, half), half)
    pair = []
    for n in range(CHUNKS):
        cols = pl.ds(n * width, width)
        pair.append(
            pltpu.make_async_remote_copy(
                src_ref=outgoing.at[:, cols],
                dst_ref=incoming.at[:, cols],
                send_sem=pair_send.at[n],
                recv_sem=pair_recv.at[n],
                device_id=sibling,
                device_id_type=MESH,
            )
        )
    for n in range(CHUNKS):
        cols = pl.ds(n * width, width)
        loads[n].wait()
        outgoing[:, cols] = jnp.dot(
            slip[other, :], green[:, cols], preferred_element_type=F32
        ).astype(BF16)
        if n == HELD:
            pl.semaphore_wait(barrier, len(partners))
            for copy in pair[:HELD]:
                copy.start()
        if n >= HELD:
            pair[n].start()
    for n in range(CHUNKS):
        cols = pl.ds(n * width, width)
        own[:, cols] = jnp.dot(
            slip[mine, :], green[:, cols], preferred_element_type=F32
        ).astype(BF16)

    for copy in pair:
        copy.wait_recv()
    lane = lax.broadcasted_iota(jnp.int32, (half, 128), 1)

    def tiles(i):
        cols = pl.ds(i * 128, 128)
        return jnp.abs(own[:, cols].astype(F32) + incoming[:, cols].astype(F32))

    rows = []
    for best in gauge_peaks(tiles, 0, here, lane):
        rows.append(jnp.max(best.T, axis=0, keepdims=True))
    peaks[...] = jnp.concatenate(rows, axis=0).astype(BF16)

    def rows_of(index, size):
        return pl.ds(pl.multiple_of(index * size, size), size)

    block = gathered.at[rows_of((z * NS_AXIS + s) * NT_AXIS + t, here), :]
    place = z * NT_AXIS + t
    plane_copies = []
    for i, partner in enumerate(plane):
        copy = pltpu.make_async_remote_copy(
            src_ref=peaks,
            dst_ref=block,
            send_sem=plane_send.at[i],
            recv_sem=plane_recv.at[place],
            device_id=partner,
            device_id_type=MESH,
        )
        copy.start()
        plane_copies.append(copy)
    pltpu.make_async_copy(peaks, block, plane_recv.at[place]).start()

    load_gauges.wait()
    load_amps.wait()
    slots = gauges.shape[0]
    listed = gauges[...]
    owner = listed >> 4
    gauge_z = owner >> 4
    gauge_y = (owner >> 2) & 3
    gauge_x = owner & 3
    gauge_s = jnp.where(core == 0, gauge_x, gauge_y)
    gauge_t = jnp.where(core == 0, gauge_y, gauge_x)
    row = (((gauge_z * 4 + gauge_s) * 4 + gauge_t) * 16 + (listed & 15)).T
    slot = lax.broadcasted_iota(jnp.int32, (slots, 1), 0)
    count = counts_ref[pl.ds(rank, 1), :]
    weight = jnp.where(slot < count, amps[...], 0.0).T
    step = 256

    def fill(i, carry):
        first = pl.multiple_of(i * step, step)
        position = lax.broadcasted_iota(jnp.int32, (tiles_here, step), 1) + first
        value = jnp.zeros((tiles_here, step), F32)
        for k in range(slots):
            value += jnp.where(row[:, k : k + 1] == position, weight[:, k : k + 1], 0.0)
        high = value.astype(BF16)
        table[0:tiles_here, pl.ds(first, step)] = high
        table[tiles_here : 2 * tiles_here, pl.ds(first, step)] = (value - high.astype(F32)).astype(BF16)
        return carry

    lax.fori_loop(0, total // step, fill, 0)

    group = NT_AXIS * here
    line_copies = []
    for i in range(NZ):
        for j in range(NT_AXIS):
            landed = gathered.at[rows_of((i * NS_AXIS + s) * NT_AXIS + j, here), :]
            pltpu.make_async_copy(landed, landed, plane_recv.at[i * NT_AXIS + j]).wait()
        part = gathered.at[rows_of(i * NS_AXIS + s, group), :]
        for d in range(1, NS_AXIS):
            copy = pltpu.make_async_remote_copy(
                src_ref=part,
                dst_ref=part,
                send_sem=line_send.at[i * (NS_AXIS - 1) + d - 1],
                recv_sem=line_recv.at[i * (NS_AXIS - 1) + d - 1],
                device_id=line[d - 1],
                device_id_type=MESH,
            )
            copy.start()
            line_copies.append(copy)
    for copy in pair + plane_copies:
        copy.wait_send()

    depth = NS_AXIS * group
    both = jnp.zeros((2 * tiles_here, half), F32)
    for i in range(NZ):
        for d in range(1, NS_AXIS):
            landed = gathered.at[rows_of(i * NS_AXIS + (s + NS_AXIS - d) % NS_AXIS, group), :]
            pltpu.make_async_copy(
                landed, landed, line_recv.at[i * (NS_AXIS - 1) + d - 1]
            ).wait()
        cut = pl.ds(i * depth, depth)
        both += jnp.dot(table[:, cut], gathered[cut, :], preferred_element_type=F32)
    out_ref[...] = (both[:tiles_here] + both[tiles_here:]).T
    for copy in line_copies:
        copy.wait_send()


def body(slip_units, slip_scales, green, coast_gauges, coast_amps, coast_counts):
    scenarios, sources = slip_units.shape
    columns = green.shape[1]
    tile_total, slots = coast_gauges.shape
    owners = lax.axis_size("rows")
    tiles_here = tile_total // owners
    half = scenarios // lax.axis_size("src")
    total = columns // NT * owners
    hbm = pl.BlockSpec(memory_space=pl.ANY)
    vmem = pl.BlockSpec(memory_space=pltpu.VMEM)
    dma = pltpu.SemaphoreType.DMA
    return pl.pallas_call(
        kernel,
        out_shape=jax.ShapeDtypeStruct((half, tiles_here), F32),
        in_specs=[hbm, vmem, hbm, hbm, hbm, vmem],
        out_specs=vmem,
        scratch_shapes=[
            pltpu.VMEM((sources, scenarios), jnp.int32),
            pltpu.VMEM((sources, columns), BF16),
            pltpu.VMEM((scenarios, sources), BF16),
            pltpu.VMEM((half, columns), BF16),
            pltpu.VMEM((half, columns), BF16),
            pltpu.VMEM((half, columns), BF16),
            pltpu.VMEM((columns // NT, half), BF16),
            pltpu.VMEM((total, half), BF16),
            pltpu.VMEM((2 * tiles_here, total), BF16),
            pltpu.VMEM((slots, tiles_here), jnp.int32),
            pltpu.VMEM((slots, tiles_here), F32),
            dma((3 + CHUNKS,)),
            dma((CHUNKS,)),
            dma((CHUNKS,)),
            dma((NZ * NT_AXIS - 1,)),
            dma((NZ * NT_AXIS,)),
            dma((NZ * (NS_AXIS - 1),)),
            dma((NZ * (NS_AXIS - 1),)),
        ],
        compiler_params=pltpu.CompilerParams(
            collective_id=0, has_side_effects=True, vmem_limit_bytes=56 * 1024 * 1024
        ),
    )(
        slip_units.T,
        slip_scales.T,
        green,
        coast_gauges.T,
        coast_amps.T,
        coast_counts.reshape(owners, tiles_here),
    )


def solution(mesh):
    in_specs = (P(None, "src"), P(None, "src"), P("src", "rows"), P(), P(), P())
    out_specs = P("src", "rows")
    return jax.shard_map(body, mesh=mesh, in_specs=in_specs, out_specs=out_specs, check_vma=False)
```

```python
import functools

import jax
import jax.numpy as jnp
from jax import lax
from jax.experimental import pallas as pl
from jax.experimental.pallas import tpu as pltpu
from jax.sharding import PartitionSpec as P

NT = 240
UBLK = 125
NX, NY, NZ = 4, 4, 8
NS_AXIS, NT_AXIS = 4, 4
DZ_ORDER = (4, 3, 5, 2, 6, 1, 7, 0)
CHUNKS = 5
HELD = 2
PIECES = 2
BF16 = jnp.bfloat16
F32 = jnp.float32
MESH = pl.DeviceIdType.MESH


def gauge_peaks(tiles, first, gauges, lane):
    peaks = []
    for g in range(first, first + gauges):
        start, end = g * NT, (g + 1) * NT
        best = None
        for tile in range(start // 128, (end + 127) // 128):
            value = tiles(tile)
            lo, hi = start - tile * 128, end - tile * 128
            if lo > 0:
                value = jnp.where(lane >= lo, value, jnp.zeros_like(value))
            if hi < 128:
                value = jnp.where(lane < hi, value, jnp.zeros_like(value))
            best = value if best is None else jnp.maximum(best, value)
        peaks.append(best)
    return peaks


def kernel(
    units_hbm, scales_hbm, green_hbm, gauges_hbm, amps_hbm, counts_hbm,
    out_ref,
    units, green, slip, own, outgoing, incoming, peaks, gathered, table,
    scales, gauges, amps, counts,
    load_sem, pair_send, pair_recv, plane_send, plane_recv, line_send, line_recv,
):
    core = lax.axis_index("src")
    rank = lax.axis_index("rows")
    sources, columns = green.shape
    part = slip.shape[0] // 4
    width = columns // CHUNKS
    here = columns // NT
    tiles_here = out_ref.shape[1]
    total = gathered.shape[1]
    x, y, z = rank % NX, (rank // NX) % NY, rank // (NX * NY)
    s = jnp.where(core == 0, x, y)
    t = jnp.where(core == 0, y, x)

    def at(s_index, t_index, z_index):
        x_index = jnp.where(core == 0, s_index, t_index)
        y_index = jnp.where(core == 0, t_index, s_index)
        return (core, (z_index * NY + y_index) * NX + x_index)

    tile_cols = pl.ds(pl.multiple_of(rank * tiles_here, 128), tiles_here)
    load_gauges = pltpu.make_async_copy(gauges_hbm.at[:, tile_cols], gauges, load_sem.at[1 + CHUNKS])
    load_amps = pltpu.make_async_copy(amps_hbm.at[:, tile_cols], amps, load_sem.at[2 + CHUNKS])
    load_gauges.start()
    load_amps.start()
    load_counts = pltpu.make_async_copy(counts_hbm, counts, load_sem.at[4 + CHUNKS])
    load_counts.start()
    load_units = pltpu.make_async_copy(units_hbm, units, load_sem.at[0])
    load_units.start()
    load_scales = pltpu.make_async_copy(scales_hbm, scales, load_sem.at[3 + CHUNKS])
    load_scales.start()
    loads = []
    for n in range(CHUNKS):
        cols = pl.ds(n * width, width)
        copy = pltpu.make_async_copy(green_hbm.at[:, cols], green.at[:, cols], load_sem.at[1 + n])
        copy.start()
        loads.append(copy)

    barrier = pltpu.get_barrier_semaphore()
    sibling = (1 - core, rank)
    plane = [
        at(s, (t + dt) % NT_AXIS, (z + dz) % NZ)
        for dz in DZ_ORDER for dt in range(NT_AXIS) if dz or dt
    ]
    line = [at((s + d) % NS_AXIS, t, z) for d in range(1, NS_AXIS)]
    partners = [sibling] + plane + line
    for partner in partners:
        pl.semaphore_signal(barrier, inc=1, device_id=partner, device_id_type=MESH)

    load_gauges.wait()
    load_amps.wait()
    load_counts.wait()
    slots = gauges.shape[0]
    listed = gauges[...]
    owner = listed >> 4
    gauge_z = owner >> 4
    gauge_y = (owner >> 2) & 3
    gauge_x = owner & 3
    gauge_s = jnp.where(core == 0, gauge_x, gauge_y)
    gauge_t = jnp.where(core == 0, gauge_y, gauge_x)
    row = (((gauge_z * 4 + gauge_s) * 4 + gauge_t) * 16 + (listed & 15)).T
    slot = lax.broadcasted_iota(jnp.int32, (slots, 1), 0)
    count = counts[pl.ds(rank, 1), :]
    weight = jnp.where(slot < count, amps[...], 0.0).T
    step = 256

    def fill(i, carry):
        first = pl.multiple_of(i * step, step)
        position = lax.broadcasted_iota(jnp.int32, (tiles_here, step), 1) + first
        value = jnp.zeros((tiles_here, step), F32)
        for k in range(slots):
            value += jnp.where(row[:, k : k + 1] == position, weight[:, k : k + 1], 0.0)
        high = value.astype(BF16)
        table[0:tiles_here, pl.ds(first, step)] = high
        table[tiles_here : 2 * tiles_here, pl.ds(first, step)] = (value - high.astype(F32)).astype(BF16)
        return carry

    lax.fori_loop(0, total // step, fill, 0)

    load_scales.wait()
    load_units.wait()
    blocks = scales.shape[0]
    for i in range(blocks):
        low, high = i * 128, min(i * 128 + 128, sources)
        scale = scales[i : i + 1, :]
        if i + 1 < blocks:
            source = lax.broadcasted_iota(jnp.int32, (high - low, 1), 0) + low
            scale = jnp.where(source < UBLK * (i + 1), scale, scales[i + 1 : i + 2, :])
        piece = units[low:high, :].astype(F32) * scale
        slip[:, low:high] = piece.astype(BF16).T

    other = pl.ds(pl.multiple_of((1 - core) * 2 * part, 2 * part), 2 * part)

    def to_sibling(h, n):
        cols = pl.ds(n * width, width)
        pltpu.make_async_remote_copy(
            src_ref=outgoing.at[h, :, cols],
            dst_ref=incoming.at[h, :, cols],
            send_sem=pair_send.at[h],
            recv_sem=pair_recv.at[h],
            device_id=sibling,
            device_id_type=MESH,
        ).start()

    for n in range(CHUNKS):
        cols = pl.ds(n * width, width)
        loads[n].wait()
        value = jnp.dot(slip[other, :], green[:, cols], preferred_element_type=F32).astype(BF16)
        outgoing[0, :, cols] = value[:part]
        outgoing[1, :, cols] = value[part:]
        if n == HELD:
            pl.semaphore_wait(barrier, len(partners))
            for h in range(2):
                for m in range(HELD):
                    to_sibling(h, m)
        if n >= HELD:
            for h in range(2):
                to_sibling(h, n)

    def rows_of(index, size):
        return pl.ds(pl.multiple_of(index * size, size), size)

    lane = lax.broadcasted_iota(jnp.int32, (part, 128), 1)
    for h in range(2):
        mine = rows_of(core * 2 + h, part)
        for n in range(CHUNKS):
            cols = pl.ds(n * width, width)
            own[h, :, cols] = jnp.dot(
                slip[mine, :], green[:, cols], preferred_element_type=F32
            ).astype(BF16)
        pltpu.make_async_copy(incoming.at[h], incoming.at[h], pair_recv.at[h]).wait()

        def tiles(i):
            cols = pl.ds(i * 128, 128)
            return jnp.abs(own[h, :, cols].astype(F32) + incoming[h, :, cols].astype(F32))

        highest = []
        for best in gauge_peaks(tiles, 0, here, lane):
            highest.append(jnp.max(best.T, axis=0, keepdims=True))
        peaks[h] = jnp.concatenate(highest, axis=0).astype(BF16)
        block = gathered.at[h, rows_of((z * NS_AXIS + s) * NT_AXIS + t, here), :]
        for partner in plane:
            pltpu.make_async_remote_copy(
                src_ref=peaks.at[h],
                dst_ref=block,
                send_sem=plane_send.at[h],
                recv_sem=plane_recv.at[h * NZ + z],
                device_id=partner,
                device_id_type=MESH,
            ).start()
        pltpu.make_async_copy(peaks.at[h], block, plane_recv.at[h * NZ + z]).start()

    group = NT_AXIS * here
    for h in range(2):
        for i in range(NZ):
            whole = gathered.at[h, rows_of(i * NS_AXIS + s, group), :]
            pltpu.make_async_copy(whole, whole, plane_recv.at[h * NZ + i]).wait()
            for d in range(1, NS_AXIS):
                pltpu.make_async_remote_copy(
                    src_ref=whole,
                    dst_ref=whole,
                    send_sem=line_send.at[h],
                    recv_sem=line_recv.at[h * NZ + i],
                    device_id=line[d - 1],
                    device_id_type=MESH,
                ).start()

    depth = NS_AXIS * group
    cut = depth * NZ // PIECES
    for h in range(2):
        both = jnp.zeros((2 * tiles_here, part), F32)
        for i in range(NZ):
            landed = gathered.at[h, pl.ds(i * depth, depth - group), :]
            pltpu.make_async_copy(landed, landed, line_recv.at[h * NZ + i]).wait()
            if (i + 1) % (NZ // PIECES) == 0:
                piece = pl.ds((i + 1) * depth - cut, cut)
                both += jnp.dot(table[:, piece], gathered[h, piece, :], preferred_element_type=F32)
        out_ref[h * part : (h + 1) * part, :] = (both[:tiles_here] + both[tiles_here:]).T

    for h in range(2):
        pltpu.make_async_copy(outgoing.at[h], outgoing.at[h], pair_send.at[h]).wait()
        sent = gathered.at[h, pl.ds(0, len(plane) * here), :]
        pltpu.make_async_copy(sent, sent, plane_send.at[h]).wait()
        sent = gathered.at[h, pl.ds(0, (NS_AXIS - 1) * group * NZ), :]
        pltpu.make_async_copy(sent, sent, line_send.at[h]).wait()


def body(slip_units, slip_scales, green, coast_gauges, coast_amps, coast_counts):
    scenarios, sources = slip_units.shape
    columns = green.shape[1]
    tile_total, slots = coast_gauges.shape
    owners = lax.axis_size("rows")
    tiles_here = tile_total // owners
    half = scenarios // lax.axis_size("src")
    total = columns // NT * owners
    hbm = pl.BlockSpec(memory_space=pl.ANY)
    vmem = pl.BlockSpec(memory_space=pltpu.VMEM)
    dma = pltpu.SemaphoreType.DMA
    return pl.pallas_call(
        kernel,
        out_shape=jax.ShapeDtypeStruct((half, tiles_here), F32),
        in_specs=[hbm] * 6,
        out_specs=vmem,
        scratch_shapes=[
            pltpu.VMEM((sources, scenarios), jnp.int32),
            pltpu.VMEM((sources, columns), BF16),
            pltpu.VMEM((scenarios, sources), BF16),
            pltpu.VMEM((2, half // 2, columns), BF16),
            pltpu.VMEM((2, half // 2, columns), BF16),
            pltpu.VMEM((2, half // 2, columns), BF16),
            pltpu.VMEM((2, columns // NT, half // 2), BF16),
            pltpu.VMEM((2, total, half // 2), BF16),
            pltpu.VMEM((2 * tiles_here, total), BF16),
            pltpu.VMEM(slip_scales.shape[::-1], F32),
            pltpu.VMEM((slots, tiles_here), jnp.int32),
            pltpu.VMEM((slots, tiles_here), F32),
            pltpu.VMEM((owners, tiles_here), jnp.int32),
            dma((5 + CHUNKS,)),
            dma((2,)),
            dma((2,)),
            dma((2,)),
            dma((2 * NZ,)),
            dma((2,)),
            dma((2 * NZ,)),
        ],
        compiler_params=pltpu.CompilerParams(
            collective_id=0, has_side_effects=True, vmem_limit_bytes=58 * 1024 * 1024
        ),
    )(
        slip_units.T,
        slip_scales.T,
        green,
        coast_gauges.T,
        coast_amps.T,
        coast_counts.reshape(owners, tiles_here),
    )


def solution(mesh):
    in_specs = (P(None, "src"), P(None, "src"), P("src", "rows"), P(), P(), P())
    out_specs = P("src", "rows")
    return jax.shard_map(body, mesh=mesh, in_specs=in_specs, out_specs=out_specs, check_vma=False)
```

```python
import functools

import jax
import jax.numpy as jnp
from jax import lax
from jax.experimental import pallas as pl
from jax.experimental.pallas import tpu as pltpu
from jax.sharding import PartitionSpec as P

NT = 240
UBLK = 125
NX, NY, NZ = 4, 4, 8
NS_AXIS, NT_AXIS = 4, 4
CHUNKS = 5
HELD = 1
PIECES = 2
BF16 = jnp.bfloat16
F32 = jnp.float32
MESH = pl.DeviceIdType.MESH


def gauge_peaks(tiles, first, gauges, lane):
    peaks = []
    for g in range(first, first + gauges):
        start, end = g * NT, (g + 1) * NT
        best = None
        for tile in range(start // 128, (end + 127) // 128):
            value = tiles(tile)
            lo, hi = start - tile * 128, end - tile * 128
            if lo > 0:
                value = jnp.where(lane >= lo, value, jnp.zeros_like(value))
            if hi < 128:
                value = jnp.where(lane < hi, value, jnp.zeros_like(value))
            best = value if best is None else jnp.maximum(best, value)
        peaks.append(best)
    return peaks


def kernel(
    units_hbm, scales_hbm, green_hbm, gauges_hbm, amps_hbm, counts_hbm,
    out_ref,
    units, green, slip, own, outgoing, incoming, peaks, gathered, table,
    scales, gauges, amps, counts,
    load_sem, pair_send, pair_recv, plane_send, plane_recv, line_send, line_recv,
):
    core = lax.axis_index("src")
    rank = lax.axis_index("rows")
    sources, columns = green.shape
    part = slip.shape[0] // 4
    width = columns // CHUNKS
    here = columns // NT
    tiles_here = out_ref.shape[1]
    total = gathered.shape[1]
    x, y, z = rank % NX, (rank // NX) % NY, rank // (NX * NY)
    s = jnp.where(core == 0, x, y)
    t = jnp.where(core == 0, y, x)

    def at(s_index, t_index, z_index):
        x_index = jnp.where(core == 0, s_index, t_index)
        y_index = jnp.where(core == 0, t_index, s_index)
        return (core, (z_index * NY + y_index) * NX + x_index)

    tile_cols = pl.ds(pl.multiple_of(rank * tiles_here, 128), tiles_here)
    load_gauges = pltpu.make_async_copy(gauges_hbm.at[:, tile_cols], gauges, load_sem.at[1 + CHUNKS])
    load_amps = pltpu.make_async_copy(amps_hbm.at[:, tile_cols], amps, load_sem.at[2 + CHUNKS])
    load_gauges.start()
    load_amps.start()
    load_counts = pltpu.make_async_copy(counts_hbm, counts, load_sem.at[4 + CHUNKS])
    load_counts.start()
    load_units = pltpu.make_async_copy(units_hbm, units, load_sem.at[0])
    load_units.start()
    load_scales = pltpu.make_async_copy(scales_hbm, scales, load_sem.at[3 + CHUNKS])
    load_scales.start()
    loads = []
    for n in range(CHUNKS):
        cols = pl.ds(n * width, width)
        copy = pltpu.make_async_copy(green_hbm.at[:, cols], green.at[:, cols], load_sem.at[1 + n])
        copy.start()
        loads.append(copy)

    barrier = pltpu.get_barrier_semaphore()
    sibling = (1 - core, rank)
    offsets = [(dz, dt) for dz in range(NZ) for dt in range(NT_AXIS) if dz or dt]
    offsets.sort(key=lambda o: -(min(o[0], NZ - o[0]) + min(o[1], NT_AXIS - o[1])))
    plane = [at(s, (t + dt) % NT_AXIS, (z + dz) % NZ) for dz, dt in offsets]
    line = [at((s + d) % NS_AXIS, t, z) for d in (2, 1, 3)]
    partners = [sibling] + plane + line
    for partner in partners:
        pl.semaphore_signal(barrier, inc=1, device_id=partner, device_id_type=MESH)

    load_scales.wait()
    load_units.wait()
    blocks = scales.shape[0]
    for i in range(blocks):
        low, high = i * 128, min(i * 128 + 128, sources)
        scale = scales[i : i + 1, :]
        if i + 1 < blocks:
            source = lax.broadcasted_iota(jnp.int32, (high - low, 1), 0) + low
            scale = jnp.where(source < UBLK * (i + 1), scale, scales[i + 1 : i + 2, :])
        piece = units[low:high, :].astype(F32) * scale
        slip[:, low:high] = piece.astype(BF16).T

    other = pl.ds(pl.multiple_of((1 - core) * 2 * part, 2 * part), 2 * part)

    def to_sibling(h, n):
        cols = pl.ds(n * width, width)
        pltpu.make_async_remote_copy(
            src_ref=outgoing.at[h, :, cols],
            dst_ref=incoming.at[h, :, cols],
            send_sem=pair_send.at[h],
            recv_sem=pair_recv.at[h],
            device_id=sibling,
            device_id_type=MESH,
        ).start()

    for n in range(CHUNKS):
        cols = pl.ds(n * width, width)
        loads[n].wait()
        value = jnp.dot(slip[other, :], green[:, cols], preferred_element_type=F32).astype(BF16)
        outgoing[0, :, cols] = value[:part]
        outgoing[1, :, cols] = value[part:]
        if n == HELD:
            pl.semaphore_wait(barrier, len(partners))
            for h in range(2):
                for m in range(HELD):
                    to_sibling(h, m)
        if n >= HELD:
            for h in range(2):
                to_sibling(h, n)

    def rows_of(index, size):
        return pl.ds(pl.multiple_of(index * size, size), size)

    lane = lax.broadcasted_iota(jnp.int32, (part, 128), 1)
    for h in range(2):
        mine = rows_of(core * 2 + h, part)
        for n in range(CHUNKS):
            cols = pl.ds(n * width, width)
            own[h, :, cols] = jnp.dot(
                slip[mine, :], green[:, cols], preferred_element_type=F32
            ).astype(BF16)
        pltpu.make_async_copy(incoming.at[h], incoming.at[h], pair_recv.at[h]).wait()

        def tiles(i):
            cols = pl.ds(i * 128, 128)
            return jnp.abs(own[h, :, cols].astype(F32) + incoming[h, :, cols].astype(F32))

        highest = []
        for best in gauge_peaks(tiles, 0, here, lane):
            highest.append(jnp.max(best.T, axis=0, keepdims=True))
        peaks[h] = jnp.concatenate(highest, axis=0).astype(BF16)
        block = gathered.at[h, rows_of((z * NS_AXIS + s) * NT_AXIS + t, here), :]
        for partner in plane:
            pltpu.make_async_remote_copy(
                src_ref=peaks.at[h],
                dst_ref=block,
                send_sem=plane_send.at[h],
                recv_sem=plane_recv.at[h * NZ + z],
                device_id=partner,
                device_id_type=MESH,
            ).start()
        pltpu.make_async_copy(peaks.at[h], block, plane_recv.at[h * NZ + z]).start()

    group = NT_AXIS * here
    for h in range(2):
        for i in range(NZ):
            whole = gathered.at[h, rows_of(i * NS_AXIS + s, group), :]
            pltpu.make_async_copy(whole, whole, plane_recv.at[h * NZ + i]).wait()
            for partner in line:
                pltpu.make_async_remote_copy(
                    src_ref=whole,
                    dst_ref=whole,
                    send_sem=line_send.at[h],
                    recv_sem=line_recv.at[h * NZ + i],
                    device_id=partner,
                    device_id_type=MESH,
                ).start()

    load_gauges.wait()
    load_amps.wait()
    load_counts.wait()
    slots = gauges.shape[0]
    listed = gauges[...]
    owner = listed >> 4
    gauge_z = owner >> 4
    gauge_y = (owner >> 2) & 3
    gauge_x = owner & 3
    gauge_s = jnp.where(core == 0, gauge_x, gauge_y)
    gauge_t = jnp.where(core == 0, gauge_y, gauge_x)
    row = (((gauge_z * 4 + gauge_s) * 4 + gauge_t) * 16 + (listed & 15)).T
    slot = lax.broadcasted_iota(jnp.int32, (slots, 1), 0)
    count = counts[pl.ds(rank, 1), :]
    weight = jnp.where(slot < count, amps[...], 0.0).T
    step = 256

    def fill(i, carry):
        first = pl.multiple_of(i * step, step)
        position = lax.broadcasted_iota(jnp.int32, (tiles_here, step), 1) + first
        value = jnp.zeros((tiles_here, step), F32)
        for k in range(slots):
            value += jnp.where(row[:, k : k + 1] == position, weight[:, k : k + 1], 0.0)
        high = value.astype(BF16)
        table[0:tiles_here, pl.ds(first, step)] = high
        table[tiles_here : 2 * tiles_here, pl.ds(first, step)] = (value - high.astype(F32)).astype(BF16)
        return carry

    lax.fori_loop(0, total // step, fill, 0)

    depth = NS_AXIS * group
    cut = depth * NZ // PIECES
    for h in range(2):
        both = jnp.zeros((2 * tiles_here, part), F32)
        for i in range(NZ):
            landed = gathered.at[h, pl.ds(i * depth, depth - group), :]
            pltpu.make_async_copy(landed, landed, line_recv.at[h * NZ + i]).wait()
            if (i + 1) % (NZ // PIECES) == 0:
                piece = pl.ds((i + 1) * depth - cut, cut)
                both += jnp.dot(table[:, piece], gathered[h, piece, :], preferred_element_type=F32)
        out_ref[h * part : (h + 1) * part, :] = (both[:tiles_here] + both[tiles_here:]).T

    for h in range(2):
        pltpu.make_async_copy(outgoing.at[h], outgoing.at[h], pair_send.at[h]).wait()
        sent = gathered.at[h, pl.ds(0, len(plane) * here), :]
        pltpu.make_async_copy(sent, sent, plane_send.at[h]).wait()
        sent = gathered.at[h, pl.ds(0, (NS_AXIS - 1) * group * NZ), :]
        pltpu.make_async_copy(sent, sent, line_send.at[h]).wait()


def body(slip_units, slip_scales, green, coast_gauges, coast_amps, coast_counts):
    scenarios, sources = slip_units.shape
    columns = green.shape[1]
    tile_total, slots = coast_gauges.shape
    owners = lax.axis_size("rows")
    tiles_here = tile_total // owners
    half = scenarios // lax.axis_size("src")
    total = columns // NT * owners
    hbm = pl.BlockSpec(memory_space=pl.ANY)
    vmem = pl.BlockSpec(memory_space=pltpu.VMEM)
    dma = pltpu.SemaphoreType.DMA
    return pl.pallas_call(
        kernel,
        out_shape=jax.ShapeDtypeStruct((half, tiles_here), F32),
        in_specs=[hbm] * 6,
        out_specs=vmem,
        scratch_shapes=[
            pltpu.VMEM((sources, scenarios), jnp.int32),
            pltpu.VMEM((sources, columns), BF16),
            pltpu.VMEM((scenarios, sources), BF16),
            pltpu.VMEM((2, half // 2, columns), BF16),
            pltpu.VMEM((2, half // 2, columns), BF16),
            pltpu.VMEM((2, half // 2, columns), BF16),
            pltpu.VMEM((2, columns // NT, half // 2), BF16),
            pltpu.VMEM((2, total, half // 2), BF16),
            pltpu.VMEM((2 * tiles_here, total), BF16),
            pltpu.VMEM(slip_scales.shape[::-1], F32),
            pltpu.VMEM((slots, tiles_here), jnp.int32),
            pltpu.VMEM((slots, tiles_here), F32),
            pltpu.VMEM((owners, tiles_here), jnp.int32),
            dma((5 + CHUNKS,)),
            dma((2,)),
            dma((2,)),
            dma((2,)),
            dma((2 * NZ,)),
            dma((2,)),
            dma((2 * NZ,)),
        ],
        compiler_params=pltpu.CompilerParams(
            collective_id=0, has_side_effects=True, vmem_limit_bytes=58 * 1024 * 1024
        ),
    )(
        slip_units.T,
        slip_scales.T,
        green,
        coast_gauges.T,
        coast_amps.T,
        coast_counts.reshape(owners, tiles_here),
    )


def solution(mesh):
    in_specs = (P(None, "src"), P(None, "src"), P("src", "rows"), P(), P(), P())
    out_specs = P("src", "rows")
    return jax.shard_map(body, mesh=mesh, in_specs=in_specs, out_specs=out_specs, check_vma=False)
```

```python
import functools

import jax
import jax.numpy as jnp
from jax import lax
from jax.experimental import pallas as pl
from jax.experimental.pallas import tpu as pltpu
from jax.sharding import PartitionSpec as P

NT = 240
UBLK = 125
NX, NY, NZ = 4, 4, 8
NS_AXIS, NT_AXIS = 4, 4
CHUNKS = 5
HELD = 2
PIECES = 4
BF16 = jnp.bfloat16
F32 = jnp.float32
MESH = pl.DeviceIdType.MESH


def gauge_peaks(tiles, first, gauges, lane):
    peaks = []
    for g in range(first, first + gauges):
        start, end = g * NT, (g + 1) * NT
        best = None
        for tile in range(start // 128, (end + 127) // 128):
            value = tiles(tile)
            lo, hi = start - tile * 128, end - tile * 128
            if lo > 0:
                value = jnp.where(lane >= lo, value, jnp.zeros_like(value))
            if hi < 128:
                value = jnp.where(lane < hi, value, jnp.zeros_like(value))
            best = value if best is None else jnp.maximum(best, value)
        peaks.append(best)
    return peaks


def kernel(
    units_hbm, scales_hbm, green_hbm, gauges_hbm, amps_hbm, counts_hbm,
    out_ref,
    units, green, slip, own, outgoing, incoming, peaks, gathered, table,
    scales, gauges, amps, counts,
    load_sem, pair_send, pair_recv, plane_send, plane_recv, line_send, line_recv,
):
    core = lax.axis_index("src")
    rank = lax.axis_index("rows")
    sources, columns = green.shape
    part = slip.shape[0] // 4
    width = columns // CHUNKS
    here = columns // NT
    tiles_here = out_ref.shape[1]
    total = gathered.shape[1]
    x, y, z = rank % NX, (rank // NX) % NY, rank // (NX * NY)
    s = jnp.where(core == 0, x, y)
    t = jnp.where(core == 0, y, x)

    def at(s_index, t_index, z_index):
        x_index = jnp.where(core == 0, s_index, t_index)
        y_index = jnp.where(core == 0, t_index, s_index)
        return (core, (z_index * NY + y_index) * NX + x_index)

    tile_cols = pl.ds(pl.multiple_of(rank * tiles_here, 128), tiles_here)
    load_gauges = pltpu.make_async_copy(gauges_hbm.at[:, tile_cols], gauges, load_sem.at[1 + CHUNKS])
    load_amps = pltpu.make_async_copy(amps_hbm.at[:, tile_cols], amps, load_sem.at[2 + CHUNKS])
    load_gauges.start()
    load_amps.start()
    load_counts = pltpu.make_async_copy(counts_hbm, counts, load_sem.at[4 + CHUNKS])
    load_counts.start()
    load_units = pltpu.make_async_copy(units_hbm, units, load_sem.at[0])
    load_units.start()
    load_scales = pltpu.make_async_copy(scales_hbm, scales, load_sem.at[3 + CHUNKS])
    load_scales.start()
    loads = []
    for n in range(CHUNKS):
        cols = pl.ds(n * width, width)
        copy = pltpu.make_async_copy(green_hbm.at[:, cols], green.at[:, cols], load_sem.at[1 + n])
        copy.start()
        loads.append(copy)

    barrier = pltpu.get_barrier_semaphore()
    sibling = (1 - core, rank)
    offsets = [(dz, dt) for dz in range(NZ) for dt in range(NT_AXIS) if dz or dt]
    offsets.sort(key=lambda o: -(min(o[0], NZ - o[0]) + min(o[1], NT_AXIS - o[1])))
    plane = [at(s, (t + dt) % NT_AXIS, (z + dz) % NZ) for dz, dt in offsets]
    line = [at((s + d) % NS_AXIS, t, z) for d in (2, 1, 3)]
    partners = [sibling] + plane + line
    for partner in partners:
        pl.semaphore_signal(barrier, inc=1, device_id=partner, device_id_type=MESH)

    load_scales.wait()
    load_units.wait()
    blocks = scales.shape[0]
    for i in range(blocks):
        low, high = i * 128, min(i * 128 + 128, sources)
        scale = scales[i : i + 1, :]
        if i + 1 < blocks:
            source = lax.broadcasted_iota(jnp.int32, (high - low, 1), 0) + low
            scale = jnp.where(source < UBLK * (i + 1), scale, scales[i + 1 : i + 2, :])
        piece = units[low:high, :].astype(F32) * scale
        slip[:, low:high] = piece.astype(BF16).T

    other = pl.ds(pl.multiple_of((1 - core) * 2 * part, 2 * part), 2 * part)

    def to_sibling(h, n):
        cols = pl.ds(n * width, width)
        pltpu.make_async_remote_copy(
            src_ref=outgoing.at[h, :, cols],
            dst_ref=incoming.at[h, :, cols],
            send_sem=pair_send.at[h],
            recv_sem=pair_recv.at[h],
            device_id=sibling,
            device_id_type=MESH,
        ).start()

    for n in range(CHUNKS):
        cols = pl.ds(n * width, width)
        loads[n].wait()
        value = jnp.dot(slip[other, :], green[:, cols], preferred_element_type=F32).astype(BF16)
        outgoing[0, :, cols] = value[:part]
        outgoing[1, :, cols] = value[part:]
        if n == HELD:
            pl.semaphore_wait(barrier, len(partners))
            for m in range(HELD):
                to_sibling(0, m)
        if n >= HELD:
            to_sibling(0, n)
    for n in range(CHUNKS):
        to_sibling(1, n)

    def rows_of(index, size):
        return pl.ds(pl.multiple_of(index * size, size), size)

    lane = lax.broadcasted_iota(jnp.int32, (part, 128), 1)
    for h in range(2):
        mine = rows_of(core * 2 + h, part)
        for n in range(CHUNKS):
            cols = pl.ds(n * width, width)
            own[h, :, cols] = jnp.dot(
                slip[mine, :], green[:, cols], preferred_element_type=F32
            ).astype(BF16)
        pltpu.make_async_copy(incoming.at[h], incoming.at[h], pair_recv.at[h]).wait()

        def tiles(i):
            cols = pl.ds(i * 128, 128)
            value = own[h, :, cols].astype(F32) + incoming[h, :, cols].astype(F32)
            return jnp.abs(value).astype(BF16)

        highest = []
        for best in gauge_peaks(tiles, 0, here, lane):
            turned = best.T
            top = turned[0:16]
            for i in range(16, 128, 16):
                top = jnp.maximum(top, turned[i : i + 16])
            highest.append(jnp.max(top.astype(F32), axis=0, keepdims=True))
        peaks[h] = jnp.concatenate(highest, axis=0).astype(BF16)
        block = gathered.at[h, rows_of((z * NS_AXIS + s) * NT_AXIS + t, here), :]
        for partner in plane:
            pltpu.make_async_remote_copy(
                src_ref=peaks.at[h],
                dst_ref=block,
                send_sem=plane_send.at[h],
                recv_sem=plane_recv.at[h * NZ + z],
                device_id=partner,
                device_id_type=MESH,
            ).start()
        pltpu.make_async_copy(peaks.at[h], block, plane_recv.at[h * NZ + z]).start()

    group = NT_AXIS * here
    for h in range(2):
        for i in range(NZ):
            whole = gathered.at[h, rows_of(i * NS_AXIS + s, group), :]
            pltpu.make_async_copy(whole, whole, plane_recv.at[h * NZ + i]).wait()
            for partner in line:
                pltpu.make_async_remote_copy(
                    src_ref=whole,
                    dst_ref=whole,
                    send_sem=line_send.at[h],
                    recv_sem=line_recv.at[h * NZ + i],
                    device_id=partner,
                    device_id_type=MESH,
                ).start()

    load_gauges.wait()
    load_amps.wait()
    load_counts.wait()
    slots = gauges.shape[0]
    listed = gauges[...]
    owner = listed >> 4
    gauge_z = owner >> 4
    gauge_y = (owner >> 2) & 3
    gauge_x = owner & 3
    gauge_s = jnp.where(core == 0, gauge_x, gauge_y)
    gauge_t = jnp.where(core == 0, gauge_y, gauge_x)
    row = (((gauge_z * 4 + gauge_s) * 4 + gauge_t) * 16 + (listed & 15)).T
    slot = lax.broadcasted_iota(jnp.int32, (slots, 1), 0)
    count = counts[pl.ds(rank, 1), :]
    weight = jnp.where(slot < count, amps[...], 0.0).T
    step = 256

    def fill(i, carry):
        first = pl.multiple_of(i * step, step)
        position = lax.broadcasted_iota(jnp.int32, (tiles_here, step), 1) + first
        value = jnp.zeros((tiles_here, step), F32)
        for k in range(slots):
            value += jnp.where(row[:, k : k + 1] == position, weight[:, k : k + 1], 0.0)
        high = value.astype(BF16)
        table[0:tiles_here, pl.ds(first, step)] = high
        table[tiles_here : 2 * tiles_here, pl.ds(first, step)] = (value - high.astype(F32)).astype(BF16)
        return carry

    lax.fori_loop(0, total // step, fill, 0)

    depth = NS_AXIS * group
    cut = depth * NZ // PIECES
    for h in range(2):
        both = jnp.zeros((2 * tiles_here, part), F32)
        for i in range(NZ):
            landed = gathered.at[h, pl.ds(i * depth, depth - group), :]
            pltpu.make_async_copy(landed, landed, line_recv.at[h * NZ + i]).wait()
            if (i + 1) % (NZ // PIECES) == 0:
                piece = pl.ds((i + 1) * depth - cut, cut)
                both += jnp.dot(table[:, piece], gathered[h, piece, :], preferred_element_type=F32)
        out_ref[h * part : (h + 1) * part, :] = (both[:tiles_here] + both[tiles_here:]).T

    for h in range(2):
        pltpu.make_async_copy(outgoing.at[h], outgoing.at[h], pair_send.at[h]).wait()
        sent = gathered.at[h, pl.ds(0, len(plane) * here), :]
        pltpu.make_async_copy(sent, sent, plane_send.at[h]).wait()
        sent = gathered.at[h, pl.ds(0, (NS_AXIS - 1) * group * NZ), :]
        pltpu.make_async_copy(sent, sent, line_send.at[h]).wait()


def body(slip_units, slip_scales, green, coast_gauges, coast_amps, coast_counts):
    scenarios, sources = slip_units.shape
    columns = green.shape[1]
    tile_total, slots = coast_gauges.shape
    owners = lax.axis_size("rows")
    tiles_here = tile_total // owners
    half = scenarios // lax.axis_size("src")
    total = columns // NT * owners
    hbm = pl.BlockSpec(memory_space=pl.ANY)
    vmem = pl.BlockSpec(memory_space=pltpu.VMEM)
    dma = pltpu.SemaphoreType.DMA
    return pl.pallas_call(
        kernel,
        out_shape=jax.ShapeDtypeStruct((half, tiles_here), F32),
        in_specs=[hbm] * 6,
        out_specs=vmem,
        scratch_shapes=[
            pltpu.VMEM((sources, scenarios), jnp.int32),
            pltpu.VMEM((sources, columns), BF16),
            pltpu.VMEM((scenarios, sources), BF16),
            pltpu.VMEM((2, half // 2, columns), BF16),
            pltpu.VMEM((2, half // 2, columns), BF16),
            pltpu.VMEM((2, half // 2, columns), BF16),
            pltpu.VMEM((2, columns // NT, half // 2), BF16),
            pltpu.VMEM((2, total, half // 2), BF16),
            pltpu.VMEM((2 * tiles_here, total), BF16),
            pltpu.VMEM(slip_scales.shape[::-1], F32),
            pltpu.VMEM((slots, tiles_here), jnp.int32),
            pltpu.VMEM((slots, tiles_here), F32),
            pltpu.VMEM((owners, tiles_here), jnp.int32),
            dma((5 + CHUNKS,)),
            dma((2,)),
            dma((2,)),
            dma((2,)),
            dma((2 * NZ,)),
            dma((2,)),
            dma((2 * NZ,)),
        ],
        compiler_params=pltpu.CompilerParams(
            collective_id=0, has_side_effects=True, vmem_limit_bytes=58 * 1024 * 1024
        ),
    )(
        slip_units.T,
        slip_scales.T,
        green,
        coast_gauges.T,
        coast_amps.T,
        coast_counts.reshape(owners, tiles_here),
    )


def solution(mesh):
    in_specs = (P(None, "src"), P(None, "src"), P("src", "rows"), P(), P(), P())
    out_specs = P("src", "rows")
    return jax.shard_map(body, mesh=mesh, in_specs=in_specs, out_specs=out_specs, check_vma=False)
```

```python
import functools

import jax
import jax.numpy as jnp
from jax import lax
from jax.experimental import pallas as pl
from jax.experimental.pallas import tpu as pltpu
from jax.sharding import PartitionSpec as P

NT = 240
UBLK = 125
NX, NY, NZ = 4, 4, 8
NS_AXIS, NT_AXIS = 4, 4
CHUNKS = 5
HELD = 2
PIECES = 4
BF16 = jnp.bfloat16
F32 = jnp.float32
MESH = pl.DeviceIdType.MESH


def gauge_peaks(tiles, first, gauges, lane):
    peaks = []
    for g in range(first, first + gauges):
        start, end = g * NT, (g + 1) * NT
        best = None
        for tile in range(start // 128, (end + 127) // 128):
            value = tiles(tile)
            lo, hi = start - tile * 128, end - tile * 128
            if lo > 0:
                value = jnp.where(lane >= lo, value, jnp.zeros_like(value))
            if hi < 128:
                value = jnp.where(lane < hi, value, jnp.zeros_like(value))
            best = value if best is None else jnp.maximum(best, value)
        peaks.append(best)
    return peaks


def kernel(
    units_hbm, scales_hbm, green_hbm, gauges_hbm, amps_hbm, counts_hbm,
    out_ref,
    units, green, slip, own, outgoing, incoming, peaks, gathered, table,
    scales, gauges, amps, counts,
    load_sem, pair_send, pair_recv, plane_send, plane_recv, line_send, line_recv,
):
    core = lax.axis_index("src")
    rank = lax.axis_index("rows")
    sources, columns = green.shape
    part = slip.shape[0] // 4
    width = columns // CHUNKS
    here = columns // NT
    tiles_here = out_ref.shape[1]
    total = gathered.shape[1]
    x, y, z = rank % NX, (rank // NX) % NY, rank // (NX * NY)
    s = jnp.where(core == 0, x, y)
    t = jnp.where(core == 0, y, x)

    def at(s_index, t_index, z_index):
        x_index = jnp.where(core == 0, s_index, t_index)
        y_index = jnp.where(core == 0, t_index, s_index)
        return (core, (z_index * NY + y_index) * NX + x_index)

    tile_cols = pl.ds(pl.multiple_of(rank * tiles_here, 128), tiles_here)
    load_gauges = pltpu.make_async_copy(gauges_hbm.at[:, tile_cols], gauges, load_sem.at[1 + CHUNKS])
    load_amps = pltpu.make_async_copy(amps_hbm.at[:, tile_cols], amps, load_sem.at[2 + CHUNKS])
    load_gauges.start()
    load_amps.start()
    load_counts = pltpu.make_async_copy(counts_hbm, counts, load_sem.at[4 + CHUNKS])
    load_counts.start()
    load_units = []
    for i, (low, high) in enumerate(((0, 512), (512, sources))):
        copy = pltpu.make_async_copy(
            units_hbm.at[low:high, :], units.at[low:high, :], load_sem.at[(5 + CHUNKS) * i]
        )
        copy.start()
        load_units.append(copy)
    load_scales = pltpu.make_async_copy(scales_hbm, scales, load_sem.at[3 + CHUNKS])
    load_scales.start()
    loads = []
    for n in range(CHUNKS):
        cols = pl.ds(n * width, width)
        copy = pltpu.make_async_copy(green_hbm.at[:, cols], green.at[:, cols], load_sem.at[1 + n])
        copy.start()
        loads.append(copy)

    barrier = pltpu.get_barrier_semaphore()
    sibling = (1 - core, rank)
    offsets = [(dz, dt) for dz in range(NZ) for dt in range(NT_AXIS) if dz or dt]
    offsets.sort(key=lambda o: -(min(o[0], NZ - o[0]) + min(o[1], NT_AXIS - o[1])))
    plane = [at(s, (t + dt) % NT_AXIS, (z + dz) % NZ) for dz, dt in offsets]
    line = [at((s + d) % NS_AXIS, t, z) for d in (2, 1, 3)]
    partners = [sibling] + plane + line
    for partner in partners:
        pl.semaphore_signal(barrier, inc=1, device_id=partner, device_id_type=MESH)

    load_scales.wait()
    load_units[0].wait()
    blocks = scales.shape[0]
    for i in range(blocks):
        low, high = i * 128, min(i * 128 + 128, sources)
        if low == 512:
            load_units[1].wait()
        scale = scales[i : i + 1, :]
        if i + 1 < blocks:
            source = lax.broadcasted_iota(jnp.int32, (high - low, 1), 0) + low
            scale = jnp.where(source < UBLK * (i + 1), scale, scales[i + 1 : i + 2, :])
        piece = units[low:high, :].astype(F32) * scale
        slip[:, low:high] = piece.astype(BF16).T

    other = pl.ds(pl.multiple_of((1 - core) * 2 * part, 2 * part), 2 * part)

    def to_sibling(h, n):
        cols = pl.ds(n * width, width)
        pltpu.make_async_remote_copy(
            src_ref=outgoing.at[h, :, cols],
            dst_ref=incoming.at[h, :, cols],
            send_sem=pair_send.at[h],
            recv_sem=pair_recv.at[h],
            device_id=sibling,
            device_id_type=MESH,
        ).start()

    for n in range(CHUNKS):
        cols = pl.ds(n * width, width)
        loads[n].wait()
        value = jnp.dot(slip[other, :], green[:, cols], preferred_element_type=F32).astype(BF16)
        outgoing[0, :, cols] = value[:part]
        outgoing[1, :, cols] = value[part:]
        if n == HELD:
            pl.semaphore_wait(barrier, len(partners))
            for m in range(HELD):
                to_sibling(0, m)
        if n >= HELD:
            to_sibling(0, n)
    for n in range(CHUNKS):
        to_sibling(1, n)

    def rows_of(index, size):
        return pl.ds(pl.multiple_of(index * size, size), size)

    lane = lax.broadcasted_iota(jnp.int32, (part, 128), 1)
    for h in range(2):
        mine = rows_of(core * 2 + h, part)
        for n in range(CHUNKS):
            cols = pl.ds(n * width, width)
            own[h, :, cols] = jnp.dot(
                slip[mine, :], green[:, cols], preferred_element_type=F32
            ).astype(BF16)
        pltpu.make_async_copy(incoming.at[h], incoming.at[h], pair_recv.at[h]).wait()

        def tiles(i):
            cols = pl.ds(i * 128, 128)
            value = own[h, :, cols].astype(F32) + incoming[h, :, cols].astype(F32)
            return jnp.abs(value).astype(BF16)

        highest = []
        for best in gauge_peaks(tiles, 0, here, lane):
            turned = best.T
            top = turned[0:16]
            for i in range(16, 128, 16):
                top = jnp.maximum(top, turned[i : i + 16])
            highest.append(jnp.max(top.astype(F32), axis=0, keepdims=True))
        peaks[h] = jnp.concatenate(highest, axis=0).astype(BF16)
        block = gathered.at[h, rows_of((z * NS_AXIS + s) * NT_AXIS + t, here), :]
        for partner in plane:
            pltpu.make_async_remote_copy(
                src_ref=peaks.at[h],
                dst_ref=block,
                send_sem=plane_send.at[h],
                recv_sem=plane_recv.at[h * NZ + z],
                device_id=partner,
                device_id_type=MESH,
            ).start()
        pltpu.make_async_copy(peaks.at[h], block, plane_recv.at[h * NZ + z]).start()

    group = NT_AXIS * here
    for h in range(2):
        for i in range(NZ):
            whole = gathered.at[h, rows_of(i * NS_AXIS + s, group), :]
            pltpu.make_async_copy(whole, whole, plane_recv.at[h * NZ + i]).wait()
            for partner in line:
                pltpu.make_async_remote_copy(
                    src_ref=whole,
                    dst_ref=whole,
                    send_sem=line_send.at[h],
                    recv_sem=line_recv.at[h * NZ + i],
                    device_id=partner,
                    device_id_type=MESH,
                ).start()

    load_gauges.wait()
    load_amps.wait()
    load_counts.wait()
    slots = gauges.shape[0]
    listed = gauges[...]
    owner = listed >> 4
    gauge_z = owner >> 4
    gauge_y = (owner >> 2) & 3
    gauge_x = owner & 3
    gauge_s = jnp.where(core == 0, gauge_x, gauge_y)
    gauge_t = jnp.where(core == 0, gauge_y, gauge_x)
    row = (((gauge_z * 4 + gauge_s) * 4 + gauge_t) * 16 + (listed & 15)).T
    slot = lax.broadcasted_iota(jnp.int32, (slots, 1), 0)
    count = counts[pl.ds(rank, 1), :]
    weight = jnp.where(slot < count, amps[...], 0.0).T
    step = 256

    def fill(i, carry):
        first = pl.multiple_of(i * step, step)
        position = lax.broadcasted_iota(jnp.int32, (tiles_here, step), 1) + first
        value = jnp.zeros((tiles_here, step), F32)
        for k in range(slots):
            value += jnp.where(row[:, k : k + 1] == position, weight[:, k : k + 1], 0.0)
        high = value.astype(BF16)
        table[0:tiles_here, pl.ds(first, step)] = high
        table[tiles_here : 2 * tiles_here, pl.ds(first, step)] = (value - high.astype(F32)).astype(BF16)
        return carry

    lax.fori_loop(0, total // step, fill, 0)

    depth = NS_AXIS * group
    cut = depth * NZ // PIECES
    for h in range(2):
        both = jnp.zeros((2 * tiles_here, part), F32)
        for i in range(NZ):
            landed = gathered.at[h, pl.ds(i * depth, depth - group), :]
            pltpu.make_async_copy(landed, landed, line_recv.at[h * NZ + i]).wait()
            if (i + 1) % (NZ // PIECES) == 0:
                piece = pl.ds((i + 1) * depth - cut, cut)
                both += jnp.dot(table[:, piece], gathered[h, piece, :], preferred_element_type=F32)
        out_ref[h * part : (h + 1) * part, :] = (both[:tiles_here] + both[tiles_here:]).T

    for h in range(2):
        pltpu.make_async_copy(outgoing.at[h], outgoing.at[h], pair_send.at[h]).wait()
        sent = gathered.at[h, pl.ds(0, len(plane) * here), :]
        pltpu.make_async_copy(sent, sent, plane_send.at[h]).wait()
        sent = gathered.at[h, pl.ds(0, (NS_AXIS - 1) * group * NZ), :]
        pltpu.make_async_copy(sent, sent, line_send.at[h]).wait()


def body(slip_units, slip_scales, green, coast_gauges, coast_amps, coast_counts):
    scenarios, sources = slip_units.shape
    columns = green.shape[1]
    tile_total, slots = coast_gauges.shape
    owners = lax.axis_size("rows")
    tiles_here = tile_total // owners
    half = scenarios // lax.axis_size("src")
    total = columns // NT * owners
    hbm = pl.BlockSpec(memory_space=pl.ANY)
    vmem = pl.BlockSpec(memory_space=pltpu.VMEM)
    dma = pltpu.SemaphoreType.DMA
    return pl.pallas_call(
        kernel,
        out_shape=jax.ShapeDtypeStruct((half, tiles_here), F32),
        in_specs=[hbm] * 6,
        out_specs=vmem,
        scratch_shapes=[
            pltpu.VMEM((sources, scenarios), jnp.int32),
            pltpu.VMEM((sources, columns), BF16),
            pltpu.VMEM((scenarios, sources), BF16),
            pltpu.VMEM((2, half // 2, columns), BF16),
            pltpu.VMEM((2, half // 2, columns), BF16),
            pltpu.VMEM((2, half // 2, columns), BF16),
            pltpu.VMEM((2, columns // NT, half // 2), BF16),
            pltpu.VMEM((2, total, half // 2), BF16),
            pltpu.VMEM((2 * tiles_here, total), BF16),
            pltpu.VMEM(slip_scales.shape[::-1], F32),
            pltpu.VMEM((slots, tiles_here), jnp.int32),
            pltpu.VMEM((slots, tiles_here), F32),
            pltpu.VMEM((owners, tiles_here), jnp.int32),
            dma((6 + CHUNKS,)),
            dma((2,)),
            dma((2,)),
            dma((2,)),
            dma((2 * NZ,)),
            dma((2,)),
            dma((2 * NZ,)),
        ],
        compiler_params=pltpu.CompilerParams(
            collective_id=0, has_side_effects=True, vmem_limit_bytes=58 * 1024 * 1024
        ),
    )(
        slip_units.T,
        slip_scales.T,
        green,
        coast_gauges.T,
        coast_amps.T,
        coast_counts.reshape(owners, tiles_here),
    )


def solution(mesh):
    in_specs = (P(None, "src"), P(None, "src"), P("src", "rows"), P(), P(), P())
    out_specs = P("src", "rows")
    return jax.shard_map(body, mesh=mesh, in_specs=in_specs, out_specs=out_specs, check_vma=False)
```
